512 devices in a mesh: slab: 16 (over x, z_hi), chan: 32 (over z_lo, y, core).
Axes of the slice: x: 4, y: 4, z: 16 (z_hi: 4, z_lo: 4; z = z_hi * 4 + z_lo), core: 2. Of those that a mesh axis runs over, the one named last changes fastest.
Arguments:
- volume: bfloat16 [32, 512, 512], P('slab', 'chan'), may hold values from -6 to 6
- kernel: bfloat16 [27, 512, 512], P(None, 'chan'), may hold values from -0.0546875 to 0.0546875
- offset: float32 [512], P('chan'), may hold values from -3 to 3
- cotangent: bfloat16 [16, 512, 128], P('slab', 'chan'), may hold values from -6 to 6
Outputs:
- pooled: bfloat16 [16, 512, 128], P('slab', 'chan')
- volume_grad: bfloat16 [32, 512, 512], P('slab', 'chan')
The draws below stay inside these ranges and needn't reach their ends.
All inputs are finite; a program needn't handle non-finite values.
Results may differ from the reference program's by a relative error of at most 0.02.
Values may be sent and summed in bfloat16 or wider, within the bound.
A program may use at most 64 MiB of HBM per device.

```python
import jax
import jax.numpy as jnp

CI = 512
CO = 512
H = 16
W = 32
DEPTH = 32
HW = 512


def shard_levels(rng, dims, split, least, top_value):
    loudness = 1.0
    for axis_at, shards_of in split:
        steps = jax.random.uniform(jax.random.fold_in(jax.random.fold_in(rng, 6), axis_at), (shards_of,), jnp.float32, least / len(split), top_value / len(split))
        loudness = loudness * jnp.repeat(jnp.exp(steps), dims[axis_at] // shards_of).reshape((-1,) + (1,) * (len(dims) - 1 - axis_at))
    return loudness


def scatter_about(key, shape, spread, limit, shards=(), held_as=jnp.bfloat16):
    entries = spread * jax.random.normal(key, shape, jnp.float32)
    if shards:
        entries = entries * shard_levels(key, shape, shards, -0.22, 0.18)
    return jnp.clip(entries, -limit, limit).astype(held_as)


def setup_inputs(seed: int = 0) -> dict:
    seeds = jax.random.split(jax.random.key(seed), 5)
    volume = scatter_about(seeds[0], (DEPTH, CI, HW), 1.0, 6.0, ((0, 16), (1, 32)))
    kernel = scatter_about(seeds[1], (27, CI, CO), (27 * CI) ** -0.5, 0.0546875, ((1, 32),))
    offset = scatter_about(seeds[2], (CO,), 0.5, 3.0, ((0, 32),), jnp.float32)
    cotangent = scatter_about(seeds[3], (DEPTH // 2, CO, HW // 4), 1.0, 6.0, ((0, 16), (1, 32)))
    return dict(volume=volume, kernel=kernel, offset=offset, cotangent=cotangent)


def shifted_plane(padded, kd, kh, kw):
    depth = padded.shape[0] - 2
    chans = padded.shape[1]
    grid = padded.reshape(depth + 2, chans, H, W)
    grid = jnp.pad(grid, ((0, 0), (0, 0), (1, 1), (1, 1)))
    return grid[kd:kd + depth, :, kh:kh + H, kw:kw + W].reshape(depth, chans, H * W)


def reference(volume, kernel, offset, cotangent):
    padded = jnp.pad(volume, ((1, 1), (0, 0), (0, 0)))
    preact = jnp.zeros((DEPTH, CO, H * W), jnp.float32)
    for kd in range(3):
        for kh in range(3):
            for kw in range(3):
                tap = 9 * kd + 3 * kh + kw
                piece = shifted_plane(padded, kd, kh, kw).astype(jnp.float32)
                preact = preact + jnp.einsum("dcp,co->dop", piece, kernel[tap].astype(jnp.float32))
    preact = preact + offset[None, :, None]
    active = jax.nn.silu(preact).reshape(DEPTH // 2, 2, CO, H // 2, 2, W // 2, 2)
    pooled = jnp.mean(active, axis=(1, 4, 6)).reshape(DEPTH // 2, CO, (H // 2) * (W // 2)).astype(jnp.bfloat16)
    upper = cotangent.astype(jnp.float32).reshape(DEPTH // 2, 1, CO, H // 2, 1, W // 2, 1) / 8.0
    upper = jnp.broadcast_to(upper, (DEPTH // 2, 2, CO, H // 2, 2, W // 2, 2)).reshape(DEPTH, CO, H * W)
    sig = jax.nn.sigmoid(preact)
    dpre = (upper * sig * (1.0 + preact * (1.0 - sig))).astype(jnp.bfloat16)
    grad_pad = jnp.pad(dpre, ((1, 1), (0, 0), (0, 0)))
    volume_grad = jnp.zeros((DEPTH, CI, H * W), jnp.float32)
    for kd in range(3):
        for kh in range(3):
            for kw in range(3):
                tap = 9 * kd + 3 * kh + kw
                piece = shifted_plane(grad_pad, kd, kh, kw).astype(jnp.float32)
                volume_grad = volume_grad + jnp.einsum("dop,co->dcp", piece, kernel[26 - tap].astype(jnp.float32))
    return pooled, volume_grad.astype(jnp.bfloat16)
```

```python
import jax
import jax.numpy as jnp
from jax import lax
from jax.experimental import pallas as pl
from jax.experimental.pallas import tpu as pltpu
from jax.sharding import PartitionSpec as P

H = 16
W = 32
HW = H * W
ZN = 4
YN = 4
CHIPS = ZN * YN
MESH = pl.DeviceIdType.MESH
BF = jnp.bfloat16
F32 = jnp.float32


def iota(shape, dim):
    return lax.broadcasted_iota(jnp.int32, shape, dim)


def remote(src, dst, ssem, rsem, target):
    return pltpu.make_async_remote_copy(
        src_ref=src, dst_ref=dst, send_sem=ssem, recv_sem=rsem, device_id=target, device_id_type=MESH
    )


def in_grid(dh, dw):
    lane = iota((16, HW), 1)
    h, w = lane // W + dh, lane % W + dw
    return (h >= 0) & (h < H) & (w >= 0) & (w < W)


def moved(x, dh, dw):
    s = dh * W + dw
    if s == 0:
        return x
    return jnp.where(in_grid(dh, dw), pltpu.roll(x, (-s) % HW, 1), 0.0)


def dot(a, b):
    return jnp.dot(a, b, preferred_element_type=F32)


def body(
    vol_hbm, w_hbm, off_ref, cot_ref, pooled_ref, grad_ref,
    vbuf, wraw, wsend, wh, cols, acc, part, rs_recv, dp, hsend, hrecv, psend, precv,
    lsem, halo_s, halo_r, sib_s, sib_r, rs_s, rs_r, ag_s, ag_r, bh_s, bh_r, pair_s, pair_r,
):
    slab = lax.axis_index("slab")
    chan = lax.axis_index("chan")
    slabs = lax.axis_size("slab")
    core = chan % 2
    chip = chan // 2
    z, y = chip // YN, chip % YN
    up = lax.rem(slab + 1, slabs)
    down = lax.rem(slab + slabs - 1, slabs)
    sib = (slab, chan + 1 - 2 * core)

    def peer(other):
        return (slab, other * 2 + core)

    def near(s, b):
        return (s, chan if b == 0 else chan + 1 - 2 * core)

    load_v = pltpu.make_async_copy(vol_hbm, vbuf.at[pl.ds(1, 2), 0], lsem.at[0])
    load_w = pltpu.make_async_copy(w_hbm, wraw, lsem.at[1])
    load_v.start()
    load_w.start()
    barrier = pltpu.get_barrier_semaphore()
    pl.semaphore_signal(barrier, inc=1, device_id=sib, device_id_type=MESH)
    for s in (up, down):
        for b in range(2):
            pl.semaphore_signal(barrier, inc=1, device_id=near(s, b), device_id_type=MESH)

    def greet(d, _):
        pl.semaphore_signal(barrier, inc=1, device_id=peer(lax.rem(chip + d, CHIPS)), device_id_type=MESH)
        return 0

    lax.fori_loop(1, CHIPS, greet, 0)

    load_w.wait()
    wflat = wraw[...].reshape(432, 512)
    o = iota((512, 256), 0)
    r = iota((512, 256), 1)
    place = (r // 16) * 32 + r % 16
    pick_own = (o == place + 16 * core).astype(BF)
    pick_sib = (o == place + 16 * (1 - core)).astype(BF)
    wh[:, 0] = dot(wflat, pick_own).astype(BF).reshape(3, 144, 256)
    wsend[...] = dot(wflat, pick_sib).astype(BF).reshape(3, 144, 256)
    load_v.wait()

    pl.semaphore_wait(barrier, 5 + CHIPS - 1)

    halo = []
    for b in range(2):
        halo.append(remote(vbuf.at[2, 0], vbuf.at[0, b], halo_s.at[b], halo_r.at[b], near(up, b)))
        halo.append(remote(vbuf.at[1, 0], vbuf.at[3, b], halo_s.at[2 + b], halo_r.at[2 + b], near(down, b)))
    for c in halo:
        c.start()
    share_v = remote(vbuf.at[pl.ds(1, 2), 0], vbuf.at[pl.ds(1, 2), 1], sib_s.at[0], sib_r.at[0], sib)
    share_w = remote(wsend, wh.at[:, 1], sib_s.at[1], sib_r.at[1], sib)
    share_v.start()
    share_w.start()

    def columns(plane, b, keep=None):
        x = vbuf[plane, b].astype(F32)
        if keep is not None:
            x = jnp.where(keep, x, 0.0)
        for kh in range(3):
            for kw in range(3):
                row = b * 144 + (kh * 3 + kw) * 16
                cols[plane, row : row + 16] = moved(x, kh - 1, kw - 1).astype(BF)

    columns(1, 0)
    columns(2, 0)
    share_v.wait_recv()
    columns(1, 1)
    columns(2, 1)
    share_w.wait_recv()
    eye = (iota((256, 256), 0) == iota((256, 256), 1)).astype(BF)

    def turned(lo, hi):
        rows = wh[lo:hi].reshape((hi - lo) * 288, 256)
        return lax.dot_general(
            eye, rows, (((1,), (1,)), ((), ())), preferred_element_type=F32
        ).astype(BF)

    inner = cols[1:3].reshape(576, HW)
    acc[0] = dot(turned(1, 3), inner)
    acc[1] = dot(turned(0, 2), inner)
    w_lo = turned(0, 1)
    w_hi = turned(2, 3)

    for c in halo:
        c.wait_recv()
    for b in range(2):
        columns(0, b, slab > 0)
        columns(3, b, slab < slabs - 1)
    part[0] = (acc[0] + dot(w_lo, cols[0])).astype(BF)
    part[1] = (acc[1] + dot(w_hi, cols[3])).astype(BF)

    def rows(other):
        return pl.ds(pl.multiple_of(other * 16, 16), 16)

    def rs_copy(other, slot):
        return remote(part.at[:, rows(other)], rs_recv.at[slot], rs_s.at[other], rs_r.at[slot], peer(other))

    def ag_copy(other, slot):
        return remote(dp.at[:, rows(slot)], dp.at[:, rows(slot)], ag_s.at[other], ag_r.at[slot], peer(other))

    ztargets = (3 - z, lax.rem(z + 2, 4), z + 1 - 2 * lax.rem(z, 2), z)

    def spread(copy):
        for zi, zt in enumerate(ztargets):
            for dy in (2, 1, 3, 0):
                if zi < 3 or dy:
                    copy(zt * YN + lax.rem(y + dy, YN), chip).start()

    def collect(copy):
        def step(d, _):
            other = lax.rem(chip + d, CHIPS)
            copy(other, other).wait_recv()
            return 0

        lax.fori_loop(1, CHIPS, step, 0)

    def release(copy):
        def step(d, _):
            copy(lax.rem(chip + d, CHIPS), chip).wait_send()
            return 0

        lax.fori_loop(1, CHIPS, step, 0)

    spread(rs_copy)
    cell = iota((HW, 128), 0)
    coarse = iota((HW, 128), 1)
    pool = (coarse == (cell // (2 * W)) * (W // 2) + (cell % W) // 2).astype(BF)
    cell = iota((128, HW), 1)
    coarse = iota((128, HW), 0)
    unpool = (coarse == (cell // (2 * W)) * (W // 2) + (cell % W) // 2).astype(BF)
    upper = dot(cot_ref[0], unpool) * 0.125
    diag = iota((16, 16), 0) == iota((16, 16), 1)
    offset = jnp.sum(jnp.where(diag, jnp.broadcast_to(off_ref[...], (16, 16)), 0.0), axis=1, keepdims=True)
    total = part[:, rows(chip)].astype(F32)
    collect(rs_copy)

    def add(d, t):
        return t + rs_recv[lax.rem(chip + d, CHIPS)].astype(F32)

    total = lax.fori_loop(1, CHIPS, add, total)
    act = jnp.zeros((16, HW), F32)
    for d in range(2):
        v = total[d] + offset
        s = jax.nn.sigmoid(v)
        act = act + v * s
        dp[d, rows(chip)] = (upper * s * (1.0 + v * (1.0 - s))).astype(BF)
    spread(ag_copy)
    act_hi = act.astype(BF)
    act_lo = (act - act_hi.astype(F32)).astype(BF)
    pooled_ref[0] = ((dot(act_hi, pool) + dot(act_lo, pool)) * 0.125).astype(BF)
    collect(ag_copy)

    def gathered(prod):
        out = []
        for b in range(2):
            g = jnp.zeros((16, HW), F32)
            for kh in range(3):
                for kw in range(3):
                    row = b * 144 + (kh * 3 + kw) * 16
                    g = g + moved(prod[row : row + 16], 1 - kh, 1 - kw)
            out.append(g)
        return out

    flat = [wh[k].reshape(288, 256) for k in range(3)]
    dp0, dp1 = dp[0], dp[1]
    below = gathered(dot(flat[0], dp0))
    above = gathered(dot(flat[2], dp1))
    edge = []
    for b in range(2):
        hsend[0, b] = below[b].astype(BF)
        hsend[1, b] = above[b].astype(BF)
        edge.append(remote(hsend.at[0, b], hrecv.at[1, b], bh_s.at[b], bh_r.at[2 + b], near(down, b)))
        edge.append(remote(hsend.at[1, b], hrecv.at[0, b], bh_s.at[2 + b], bh_r.at[b], near(up, b)))
    for c in edge:
        c.start()
    g0 = gathered(dot(flat[0], dp1) + dot(flat[1], dp0))
    g1 = gathered(dot(flat[1], dp1) + dot(flat[2], dp0))
    psend[0] = g0[1].astype(BF)
    psend[1] = g1[1].astype(BF)
    pair = remote(psend, precv, pair_s, pair_r, sib)
    pair.start()
    pair.wait_recv()
    g0 = g0[0] + precv[0].astype(F32)
    g1 = g1[0] + precv[1].astype(F32)
    for c in edge:
        c.wait_recv()
    from_down = hrecv[0, 0].astype(F32) + hrecv[0, 1].astype(F32)
    from_up = hrecv[1, 0].astype(F32) + hrecv[1, 1].astype(F32)
    grad_ref[0] = (g0 + jnp.where(slab > 0, from_down, 0.0)).astype(BF)
    grad_ref[1] = (g1 + jnp.where(slab < slabs - 1, from_up, 0.0)).astype(BF)

    for c in halo + [share_v, share_w, pair] + edge:
        c.wait_send()
    release(rs_copy)
    release(ag_copy)


def per_device(volume, kernel, offset, cotangent):
    vmem = pl.BlockSpec(memory_space=pltpu.VMEM)
    hbm = pl.BlockSpec(memory_space=pl.ANY)
    dma = pltpu.SemaphoreType.DMA
    return pl.pallas_call(
        body,
        out_shape=(
            jax.ShapeDtypeStruct((1, 16, HW // 4), BF),
            jax.ShapeDtypeStruct((2, 16, HW), BF),
        ),
        in_specs=[hbm, hbm, vmem, vmem],
        out_specs=(vmem, vmem),
        scratch_shapes=[
            pltpu.VMEM((4, 2, 16, HW), BF),
            pltpu.VMEM((27, 16, 512), BF),
            pltpu.VMEM((3, 144, 256), BF),
            pltpu.VMEM((3, 2, 144, 256), BF),
            pltpu.VMEM((4, 288, HW), BF),
            pltpu.VMEM((2, 256, HW), F32),
            pltpu.VMEM((2, 256, HW), BF),
            pltpu.VMEM((CHIPS, 2, 16, HW), BF),
            pltpu.VMEM((2, 256, HW), BF),
            pltpu.VMEM((2, 2, 16, HW), BF),
            pltpu.VMEM((2, 2, 16, HW), BF),
            pltpu.VMEM((2, 16, HW), BF),
            pltpu.VMEM((2, 16, HW), BF),
            dma((2,)), dma((4,)), dma((4,)), dma((2,)), dma((2,)),
            dma((CHIPS,)), dma((CHIPS,)), dma((CHIPS,)), dma((CHIPS,)),
            dma((4,)), dma((4,)), dma, dma,
        ],
        compiler_params=pltpu.CompilerParams(
            collective_id=0, has_side_effects=True, vmem_limit_bytes=40 * 2**20
        ),
        name="conv_level",
    )(volume, kernel, offset.reshape(1, 16), cotangent)


def solution(mesh):
    return jax.shard_map(
        per_device,
        mesh=mesh,
        in_specs=(
            P("slab", "chan", None),
            P(None, "chan", None),
            P("chan"),
            P("slab", "chan", None),
        ),
        out_specs=(P("slab", "chan", None), P("slab", "chan", None)),
        check_vma=False,
    )
```

```python
import jax
import jax.numpy as jnp
from jax import lax
from jax.experimental import pallas as pl
from jax.experimental.pallas import tpu as pltpu
from jax.sharding import PartitionSpec as P

H = 16
W = 32
HW = H * W
YN = 4
MESH = pl.DeviceIdType.MESH
BF = jnp.bfloat16
F32 = jnp.float32


def iota(shape, dim):
    return lax.broadcasted_iota(jnp.int32, shape, dim)


def remote(src, dst, ssem, rsem, target):
    return pltpu.make_async_remote_copy(
        src_ref=src, dst_ref=dst, send_sem=ssem, recv_sem=rsem, device_id=target, device_id_type=MESH
    )


def in_grid(dh, dw):
    lane = iota((16, HW), 1)
    h, w = lane // W + dh, lane % W + dw
    return (h >= 0) & (h < H) & (w >= 0) & (w < W)


def moved(x, dh, dw):
    s = dh * W + dw
    if s == 0:
        return x
    return jnp.where(in_grid(dh, dw), pltpu.roll(x, (-s) % HW, 1), 0.0)


def dot(a, b):
    return jnp.dot(a, b, preferred_element_type=F32)


def body(
    vol_hbm, w_hbm, off_hbm, cot_hbm, pooled_ref, grad_ref,
    vbuf, wraw, off_ref, cot_ref, wsend, wh, cols, acc, part, ysum, zsend, zsum, dp, hsend, hrecv, psend, precv,
    lsem, halo_s, halo_r, sib_s, sib_r, ry_s, ry_r, rz_s, rz_r, az_s, az_r, ay_s, ay_r, bh_s, bh_r, pair_s, pair_r,
):
    slab = lax.axis_index("slab")
    chan = lax.axis_index("chan")
    slabs = lax.axis_size("slab")
    core = chan % 2
    z, y = chan // 2 // YN, chan // 2 % YN
    up = lax.rem(slab + 1, slabs)
    down = lax.rem(slab + slabs - 1, slabs)
    sib = (slab, chan + 1 - 2 * core)

    zs = (z, z + 1 - 2 * lax.rem(z, 2), lax.rem(z + 2, 4), 3 - z)

    def yto(dy):
        return (slab, (z * YN + lax.rem(y + dy, YN)) * 2 + core)

    def zto(dz):
        return (slab, (zs[dz] * YN + y) * 2 + core)

    def near(s, b):
        return (s, chan if b == 0 else chan + 1 - 2 * core)

    load_v = pltpu.make_async_copy(vol_hbm, vbuf.at[pl.ds(1, 2), 0], lsem.at[0])
    load_w = pltpu.make_async_copy(w_hbm, wraw, lsem.at[1])
    load_v.start()
    load_w.start()
    load_o = pltpu.make_async_copy(off_hbm, off_ref, lsem.at[2])
    load_c = pltpu.make_async_copy(cot_hbm, cot_ref, lsem.at[3])
    load_o.start()
    load_c.start()
    barrier = pltpu.get_barrier_semaphore()
    pl.semaphore_signal(barrier, inc=1, device_id=sib, device_id_type=MESH)
    for s in (up, down):
        for b in range(2):
            pl.semaphore_signal(barrier, inc=1, device_id=near(s, b), device_id_type=MESH)

    for d in range(1, 4):
        pl.semaphore_signal(barrier, inc=1, device_id=zto(d), device_id_type=MESH)
        pl.semaphore_signal(barrier, inc=1, device_id=yto(d), device_id_type=MESH)

    load_w.wait()
    wflat = wraw[...].reshape(432, 512)
    o = iota((512, 256), 0)
    r = iota((512, 256), 1)
    zt = 2 * ((z // 2 + r // 128) % 2) + (z % 2 + r // 64) % 2
    place = (zt * YN + r // 16 % YN) * 32 + r % 16
    pick_own = (o == place + 16 * core).astype(BF)
    pick_sib = (o == place + 16 * (1 - core)).astype(BF)
    wh[:, 0] = dot(wflat, pick_own).astype(BF).reshape(3, 144, 256)
    wsend[...] = dot(wflat, pick_sib).astype(BF).reshape(3, 144, 256)
    load_v.wait()

    pl.semaphore_wait(barrier, 11)

    halo = []
    for b in range(2):
        halo.append(remote(vbuf.at[2, 0], vbuf.at[0, b], halo_s.at[b], halo_r.at[b], near(up, b)))
        halo.append(remote(vbuf.at[1, 0], vbuf.at[3, b], halo_s.at[2 + b], halo_r.at[2 + b], near(down, b)))
    for c in halo:
        c.start()
    share_v = remote(vbuf.at[pl.ds(1, 2), 0], vbuf.at[pl.ds(1, 2), 1], sib_s.at[0], sib_r.at[0], sib)
    share_w = remote(wsend, wh.at[:, 1], sib_s.at[1], sib_r.at[1], sib)
    share_v.start()
    share_w.start()

    def columns(plane, b, keep=None):
        x = vbuf[plane, b].astype(F32)
        if keep is not None:
            x = jnp.where(keep, x, 0.0)
        for kh in range(3):
            for kw in range(3):
                row = b * 144 + (kh * 3 + kw) * 16
                cols[plane, row : row + 16] = moved(x, kh - 1, kw - 1).astype(BF)

    columns(1, 0)
    columns(2, 0)
    share_v.wait_recv()
    columns(1, 1)
    columns(2, 1)
    share_w.wait_recv()
    eye = (iota((256, 256), 0) == iota((256, 256), 1)).astype(BF)

    def turned(lo, hi):
        rows = wh[lo:hi].reshape((hi - lo) * 288, 256)
        return lax.dot_general(
            eye, rows, (((1,), (1,)), ((), ())), preferred_element_type=F32
        ).astype(BF)

    inner = cols[1:3].reshape(576, HW)
    acc[0] = dot(turned(1, 3), inner)
    acc[1] = dot(turned(0, 2), inner)
    w_lo = turned(0, 1)
    w_hi = turned(2, 3)

    for c in halo:
        c.wait_recv()
    for b in range(2):
        columns(0, b, slab > 0)
        columns(3, b, slab < slabs - 1)
    part[0] = (acc[0] + dot(w_lo, cols[0])).astype(BF)
    part[1] = (acc[1] + dot(w_hi, cols[3])).astype(BF)

    def rows(dz, yt):
        return pl.ds(pl.multiple_of(dz * 64 + yt * 16, 16), 16)

    def ry(dz, dy):
        k = dz * 4 + dy
        return remote(part.at[:, rows(dz, lax.rem(y + dy, YN))], ysum.at[dz, dy], ry_s.at[k], ry_r.at[k], yto(dy))

    def rz(dz):
        return remote(zsend.at[dz], zsum.at[dz], rz_s.at[dz], rz_r.at[dz], zto(dz))

    def az(dz):
        return remote(dp.at[:, rows(0, y)], dp.at[:, rows(dz, y)], az_s.at[dz], az_r.at[dz], zto(dz))

    def ay(dz, dy):
        k = dz * 4 + dy
        return remote(dp.at[:, rows(dz, y)], dp.at[:, rows(dz, y)], ay_s.at[k], ay_r.at[k], yto(dy))

    def ay_arrival(dz, dy):
        k = dz * 4 + dy
        here = rows(dz, lax.rem(y + 4 - dy, YN))
        return remote(dp.at[:, here], dp.at[:, here], ay_s.at[k], ay_r.at[k], yto(dy))

    for dz in (3, 2, 1, 0):
        for dy in (2, 1, 3):
            ry(dz, dy).start()
    cell = iota((HW, 128), 0)
    coarse = iota((HW, 128), 1)
    pool = (coarse == (cell // (2 * W)) * (W // 2) + (cell % W) // 2).astype(BF)
    cell = iota((128, HW), 1)
    coarse = iota((128, HW), 0)
    unpool = (coarse == (cell // (2 * W)) * (W // 2) + (cell % W) // 2).astype(BF)
    load_o.wait()
    load_c.wait()
    upper = dot(cot_ref[0], unpool) * 0.125
    diag = iota((16, 16), 0) == iota((16, 16), 1)
    offset = jnp.sum(jnp.where(diag, jnp.broadcast_to(off_ref[...], (16, 16)), 0.0), axis=1, keepdims=True)
    def ytotal(dz):
        t = part[:, rows(dz, y)].astype(F32)
        for dy in (1, 2, 3):
            ry(dz, dy).wait_recv()
        for dy in (1, 2, 3):
            t = t + ysum[dz, dy].astype(F32)
        return t

    for dz in (3, 2, 1):
        zsend[dz] = ytotal(dz).astype(BF)
        rz(dz).start()
    total = ytotal(0)
    for dz in (1, 2, 3):
        rz(dz).wait_recv()
        total = total + zsum[dz].astype(F32)
    act = jnp.zeros((16, HW), F32)
    for d in range(2):
        v = total[d] + offset
        s = jax.nn.sigmoid(v)
        act = act + v * s
        dp[d, rows(0, y)] = (upper * s * (1.0 + v * (1.0 - s))).astype(BF)
    for dz in (3, 2, 1):
        az(dz).start()
    for dy in (2, 1, 3):
        ay(0, dy).start()
    act_hi = act.astype(BF)
    act_lo = (act - act_hi.astype(F32)).astype(BF)
    pooled_ref[0] = ((dot(act_hi, pool) + dot(act_lo, pool)) * 0.125).astype(BF)
    for dz in (1, 2, 3):
        az(dz).wait_recv()
        for dy in (2, 1, 3):
            ay(dz, dy).start()
    for dz in range(4):
        for dy in (1, 2, 3):
            ay_arrival(dz, dy).wait_recv()

    def gathered(prod):
        out = []
        for b in range(2):
            g = jnp.zeros((16, HW), F32)
            for kh in range(3):
                for kw in range(3):
                    row = b * 144 + (kh * 3 + kw) * 16
                    g = g + moved(prod[row : row + 16], 1 - kh, 1 - kw)
            out.append(g)
        return out

    flat = [wh[k].reshape(288, 256) for k in range(3)]
    dp0, dp1 = dp[0], dp[1]
    below = gathered(dot(flat[0], dp0))
    above = gathered(dot(flat[2], dp1))
    edge = []
    for b in range(2):
        hsend[0, b] = below[b].astype(BF)
        hsend[1, b] = above[b].astype(BF)
        edge.append(remote(hsend.at[0, b], hrecv.at[1, b], bh_s.at[b], bh_r.at[2 + b], near(down, b)))
        edge.append(remote(hsend.at[1, b], hrecv.at[0, b], bh_s.at[2 + b], bh_r.at[b], near(up, b)))
    for c in edge:
        c.start()
    g0 = gathered(dot(flat[0], dp1) + dot(flat[1], dp0))
    g1 = gathered(dot(flat[1], dp1) + dot(flat[2], dp0))
    psend[0] = g0[1].astype(BF)
    psend[1] = g1[1].astype(BF)
    pair = remote(psend, precv, pair_s, pair_r, sib)
    pair.start()
    pair.wait_recv()
    g0 = g0[0] + precv[0].astype(F32)
    g1 = g1[0] + precv[1].astype(F32)
    for c in edge:
        c.wait_recv()
    from_down = hrecv[0, 0].astype(F32) + hrecv[0, 1].astype(F32)
    from_up = hrecv[1, 0].astype(F32) + hrecv[1, 1].astype(F32)
    grad_ref[0] = (g0 + jnp.where(slab > 0, from_down, 0.0)).astype(BF)
    grad_ref[1] = (g1 + jnp.where(slab < slabs - 1, from_up, 0.0)).astype(BF)

    for c in halo + [share_v, share_w, pair] + edge:
        c.wait_send()
    for dz in range(4):
        for dy in (1, 2, 3):
            ry(dz, dy).wait_send()
            ay(dz, dy).wait_send()
    for dz in (1, 2, 3):
        rz(dz).wait_send()
        az(dz).wait_send()


def per_device(volume, kernel, offset, cotangent):
    vmem = pl.BlockSpec(memory_space=pltpu.VMEM)
    hbm = pl.BlockSpec(memory_space=pl.ANY)
    dma = pltpu.SemaphoreType.DMA
    return pl.pallas_call(
        body,
        out_shape=(
            jax.ShapeDtypeStruct((1, 16, HW // 4), BF),
            jax.ShapeDtypeStruct((2, 16, HW), BF),
        ),
        in_specs=[hbm] * 4,
        out_specs=(vmem, vmem),
        scratch_shapes=[
            pltpu.VMEM((4, 2, 16, HW), BF),
            pltpu.VMEM((27, 16, 512), BF),
            pltpu.VMEM((1, 16), F32),
            pltpu.VMEM((1, 16, HW // 4), BF),
            pltpu.VMEM((3, 144, 256), BF),
            pltpu.VMEM((3, 2, 144, 256), BF),
            pltpu.VMEM((4, 288, HW), BF),
            pltpu.VMEM((2, 256, HW), F32),
            pltpu.VMEM((2, 256, HW), BF),
            pltpu.VMEM((4, 4, 2, 16, HW), BF),
            pltpu.VMEM((4, 2, 16, HW), BF),
            pltpu.VMEM((4, 2, 16, HW), BF),
            pltpu.VMEM((2, 256, HW), BF),
            pltpu.VMEM((2, 2, 16, HW), BF),
            pltpu.VMEM((2, 2, 16, HW), BF),
            pltpu.VMEM((2, 16, HW), BF),
            pltpu.VMEM((2, 16, HW), BF),
            dma((4,)), dma((4,)), dma((4,)), dma((2,)), dma((2,)),
            dma((16,)), dma((16,)), dma((4,)), dma((4,)),
            dma((4,)), dma((4,)), dma((16,)), dma((16,)),
            dma((4,)), dma((4,)), dma, dma,
        ],
        compiler_params=pltpu.CompilerParams(
            collective_id=0, has_side_effects=True, vmem_limit_bytes=40 * 2**20
        ),
        name="conv_level",
    )(*(pltpu.with_memory_space_constraint(a, pltpu.HBM) for a in (volume, kernel, offset.reshape(1, 16), cotangent)))


def solution(mesh):
    return jax.shard_map(
        per_device,
        mesh=mesh,
        in_specs=(
            P("slab", "chan", None),
            P(None, "chan", None),
            P("chan"),
            P("slab", "chan", None),
        ),
        out_specs=(P("slab", "chan", None), P("slab", "chan", None)),
        check_vma=False,
    )
```

```python
import jax
import jax.numpy as jnp
from jax import lax
from jax.experimental import pallas as pl
from jax.experimental.pallas import tpu as pltpu
from jax.sharding import PartitionSpec as P

H = 16
W = 32
HW = H * W
YN = 4
MESH = pl.DeviceIdType.MESH
BF = jnp.bfloat16
F32 = jnp.float32


def iota(shape, dim):
    return lax.broadcasted_iota(jnp.int32, shape, dim)


def remote(src, dst, ssem, rsem, target):
    return pltpu.make_async_remote_copy(
        src_ref=src, dst_ref=dst, send_sem=ssem, recv_sem=rsem, device_id=target, device_id_type=MESH
    )


def in_grid(dh, dw):
    lane = iota((16, HW), 1)
    h, w = lane // W + dh, lane % W + dw
    return (h >= 0) & (h < H) & (w >= 0) & (w < W)


def moved(x, dh, dw):
    s = dh * W + dw
    if s == 0:
        return x
    return jnp.where(in_grid(dh, dw), pltpu.roll(x, (-s) % HW, 1), 0.0)


def dot(a, b):
    return jnp.dot(a, b, preferred_element_type=F32)


def body(
    vol_hbm, w_hbm, off_hbm, cot_hbm, pooled_ref, grad_ref,
    vbuf, wraw, wturn, off_ref, cot_ref, wsend, wh, cols, acc, part, ysum, zsend, zsum, dp, hsend, hrecv, psend, precv,
    lsem, halo_s, halo_r, sib_s, sib_r, ry_s, ry_r, rz_s, rz_r, az_s, az_r, ay_s, ay_r, bh_s, bh_r, pair_s, pair_r,
):
    slab = lax.axis_index("slab")
    chan = lax.axis_index("chan")
    slabs = lax.axis_size("slab")
    core = chan % 2
    z, y = chan // 2 // YN, chan // 2 % YN
    up = lax.rem(slab + 1, slabs)
    down = lax.rem(slab + slabs - 1, slabs)
    sib = (slab, chan + 1 - 2 * core)

    zs = (z, z + 1 - 2 * lax.rem(z, 2), lax.rem(z + 2, 4), 3 - z)

    first = lax.rem(slab, 4) // 3
    second = 1 - first
    planes = (first, second)

    def yto(dy):
        return (slab, (z * YN + lax.rem(y + dy, YN)) * 2 + core)

    def zto(dz):
        return (slab, (zs[dz] * YN + y) * 2 + core)

    def near(s, b):
        return (s, chan if b == 0 else chan + 1 - 2 * core)

    barrier = pltpu.get_barrier_semaphore()
    pl.semaphore_signal(barrier, inc=1, device_id=sib, device_id_type=MESH)
    for s in (up, down):
        for b in range(2):
            pl.semaphore_signal(barrier, inc=1, device_id=near(s, b), device_id_type=MESH)

    for d in range(1, 4):
        pl.semaphore_signal(barrier, inc=1, device_id=zto(d), device_id_type=MESH)
        pl.semaphore_signal(barrier, inc=1, device_id=yto(d), device_id_type=MESH)

    load_v = pltpu.make_async_copy(vol_hbm, vbuf.at[pl.ds(1, 2), 0], lsem.at[0])
    load_w = pltpu.make_async_copy(w_hbm, wraw, lsem.at[1])
    load_v.start()
    load_w.start()
    load_o = pltpu.make_async_copy(off_hbm, off_ref, lsem.at[2])
    load_c = pltpu.make_async_copy(cot_hbm, cot_ref, lsem.at[3])
    load_o.start()
    load_c.start()
    pl.semaphore_wait(barrier, 11)

    halo = []
    for b in range(2):
        halo.append(remote(vol_hbm.at[1], vbuf.at[0, b], halo_s.at[b], halo_r.at[b], near(up, b)))
        halo.append(remote(vol_hbm.at[0], vbuf.at[3, b], halo_s.at[2 + b], halo_r.at[2 + b], near(down, b)))
    for c in halo:
        c.start()
    share_v = remote(vol_hbm, vbuf.at[pl.ds(1, 2), 1], sib_s.at[0], sib_r.at[0], sib)
    share_w = remote(wsend, wh.at[:, 1], sib_s.at[1], sib_r.at[1], sib)
    share_v.start()

    load_w.wait()
    wflat = wraw[...].reshape(432, 512)
    o = iota((512, 256), 0)
    r = iota((512, 256), 1)
    zt = 2 * ((z // 2 + r // 128) % 2) + (z % 2 + r // 64) % 2
    place = o - (zt * YN + r // 16 % YN) * 32 - r % 16
    wsend[...] = dot(wflat, (place == 16 * (1 - core)).astype(BF)).astype(BF).reshape(3, 144, 256)
    share_w.start()
    wh[:, 0] = dot(wflat, (place == 16 * core).astype(BF)).astype(BF).reshape(3, 144, 256)
    load_v.wait()

    def columns(plane, b, keep=None):
        x = vbuf[plane, b].astype(F32)
        if keep is not None:
            x = jnp.where(keep, x, 0.0)
        for kh in range(3):
            for kw in range(3):
                row = b * 144 + (kh * 3 + kw) * 16
                cols[plane, row : row + 16] = moved(x, kh - 1, kw - 1).astype(BF)

    columns(1, 0)
    columns(2, 0)
    share_v.wait_recv()
    columns(1, 1)
    columns(2, 1)
    share_w.wait_recv()
    eye = (iota((256, 256), 0) == iota((256, 256), 1)).astype(BF)

    def turned(lo, hi):
        rows = wh[lo:hi].reshape((hi - lo) * 288, 256)
        return lax.dot_general(
            eye, rows, (((1,), (1,)), ((), ())), preferred_element_type=F32
        ).astype(BF)

    inner = cols[1:3].reshape(576, HW)
    acc[0] = dot(turned(1, 3), inner)
    acc[1] = dot(turned(0, 2), inner)
    wturn[0] = turned(0, 1)
    wturn[1] = turned(2, 3)

    def rows(dz, yt):
        return pl.ds(pl.multiple_of(dz * 64 + yt * 16, 16), 16)

    def ry(p, dz, dy):
        k = dz * 4 + dy
        src = part.at[p, rows(dz, lax.rem(y + dy, YN))]
        return remote(src, ysum.at[p, dz, dy], ry_s.at[p, k], ry_r.at[p, k], yto(dy))

    def rz(p, dz):
        return remote(zsend.at[p, dz], zsum.at[p, dz], rz_s.at[p, dz], rz_r.at[p, dz], zto(dz))

    def az(p, dz):
        return remote(dp.at[p, rows(0, y)], dp.at[p, rows(dz, y)], az_s.at[p, dz], az_r.at[p, dz], zto(dz))

    def ay(p, dz, dy):
        k = dz * 4 + dy
        here = dp.at[p, rows(dz, y)]
        return remote(here, here, ay_s.at[p, k], ay_r.at[p, k], yto(dy))

    def ay_arrival(p, dz, dy):
        k = dz * 4 + dy
        here = dp.at[p, rows(dz, lax.rem(y + 4 - dy, YN))]
        return remote(here, here, ay_s.at[p, k], ay_r.at[p, k], yto(dy))

    def ytotal(p, dz):
        t = part[p, rows(dz, y)].astype(F32)
        for dy in (1, 2, 3):
            ry(p, dz, dy).wait_recv()
        for dy in (1, 2, 3):
            t = t + ysum[p, dz, dy].astype(F32)
        return t

    def start_sums(p):
        for b in range(2):
            k = 2 * p + b
            remote(vol_hbm.at[1 - p], vbuf.at[3 * p, b], halo_s.at[k], halo_r.at[k], near(up, b)).wait_recv()
        inside = jnp.where(p == 0, slab, slabs - 1 - slab) > 0
        for b in range(2):
            columns(3 * p, b, inside)
        part[p] = (acc[p] + dot(wturn[p], cols[3 * p])).astype(BF)
        for dz in (3, 2, 1, 0):
            for dy in (2, 1, 3):
                ry(p, dz, dy).start()

    def pass_sums(p):
        for dz in (3, 2, 1):
            zsend[p, dz] = ytotal(p, dz).astype(BF)
            rz(p, dz).start()

    start_sums(first)
    cell = iota((HW, 128), 0)
    coarse = iota((HW, 128), 1)
    pool = (coarse == (cell // (2 * W)) * (W // 2) + (cell % W) // 2).astype(BF)
    cell = iota((128, HW), 1)
    coarse = iota((128, HW), 0)
    unpool = (coarse == (cell // (2 * W)) * (W // 2) + (cell % W) // 2).astype(BF)
    load_o.wait()
    load_c.wait()
    upper = dot(cot_ref[0], unpool) * 0.125
    diag = iota((16, 16), 0) == iota((16, 16), 1)
    offset = jnp.sum(jnp.where(diag, jnp.broadcast_to(off_ref[...], (16, 16)), 0.0), axis=1, keepdims=True)
    def activate(p):
        v = ytotal(p, 0) + offset
        for dz in (1, 2, 3):
            rz(p, dz).wait_recv()
            v = v + zsum[p, dz].astype(F32)
        s = jax.nn.sigmoid(v)
        dp[p, rows(0, y)] = (upper * s * (1.0 + v * (1.0 - s))).astype(BF)
        for dz in (3, 2, 1):
            az(p, dz).start()
        for dy in (2, 1, 3):
            ay(p, 0, dy).start()
        return v * s

    def forward(p):
        for dz in (1, 2, 3):
            az(p, dz).wait_recv()
            for dy in (2, 1, 3):
                ay(p, dz, dy).start()

    start_sums(second)
    pass_sums(first)
    pass_sums(second)
    act = activate(first)
    forward(first)
    act = act + activate(second)
    forward(second)
    act_hi = act.astype(BF)
    act_lo = (act - act_hi.astype(F32)).astype(BF)
    pooled_ref[0] = ((dot(act_hi, pool) + dot(act_lo, pool)) * 0.125).astype(BF)
    def gathered(prod):
        out = []
        for b in range(2):
            g = jnp.zeros((16, HW), F32)
            for kh in range(3):
                for kw in range(3):
                    row = b * 144 + (kh * 3 + kw) * 16
                    g = g + moved(prod[row : row + 16], 1 - kh, 1 - kw)
            out.append(g)
        return out

    def edge(p, b):
        slab_to = jnp.where(p == 0, down, up)
        return remote(
            hsend.at[p, b], hrecv.at[1 - p, b], bh_s.at[2 * p + b], bh_r.at[2 * (1 - p) + b], near(slab_to, b)
        )

    for p in planes:
        for dz in range(4):
            for dy in (1, 2, 3):
                ay_arrival(p, dz, dy).wait_recv()
        beyond = gathered(dot(wh[2 * p].reshape(288, 256), dp[p]))
        for b in range(2):
            hsend[p, b] = beyond[b].astype(BF)
            edge(p, b).start()
    flat = [wh[k].reshape(288, 256) for k in range(3)]
    dp0, dp1 = dp[0], dp[1]
    g0 = gathered(dot(flat[0], dp1) + dot(flat[1], dp0))
    g1 = gathered(dot(flat[1], dp1) + dot(flat[2], dp0))
    psend[0] = g0[1].astype(BF)
    psend[1] = g1[1].astype(BF)
    pair = remote(psend, precv, pair_s, pair_r, sib)
    pair.start()
    pair.wait_recv()
    g0 = g0[0] + precv[0].astype(F32)
    g1 = g1[0] + precv[1].astype(F32)
    for p in range(2):
        for b in range(2):
            edge(p, b).wait_recv()
    from_down = hrecv[0, 0].astype(F32) + hrecv[0, 1].astype(F32)
    from_up = hrecv[1, 0].astype(F32) + hrecv[1, 1].astype(F32)
    grad_ref[0] = (g0 + jnp.where(slab > 0, from_down, 0.0)).astype(BF)
    grad_ref[1] = (g1 + jnp.where(slab < slabs - 1, from_up, 0.0)).astype(BF)

    for c in halo + [share_v, share_w, pair]:
        c.wait_send()
    for p in range(2):
        for b in range(2):
            edge(p, b).wait_send()
        for dz in range(4):
            for dy in (1, 2, 3):
                ry(p, dz, dy).wait_send()
                ay(p, dz, dy).wait_send()
        for dz in (1, 2, 3):
            rz(p, dz).wait_send()
            az(p, dz).wait_send()


def per_device(volume, kernel, offset, cotangent):
    vmem = pl.BlockSpec(memory_space=pltpu.VMEM)
    hbm = pl.BlockSpec(memory_space=pl.ANY)
    dma = pltpu.SemaphoreType.DMA
    return pl.pallas_call(
        body,
        out_shape=(
            jax.ShapeDtypeStruct((1, 16, HW // 4), BF),
            jax.ShapeDtypeStruct((2, 16, HW), BF),
        ),
        in_specs=[hbm] * 4,
        out_specs=(vmem, vmem),
        scratch_shapes=[
            pltpu.VMEM((4, 2, 16, HW), BF),
            pltpu.VMEM((27, 16, 512), BF),
            pltpu.VMEM((2, 256, 288), BF),
            pltpu.VMEM((1, 16), F32),
            pltpu.VMEM((1, 16, HW // 4), BF),
            pltpu.VMEM((3, 144, 256), BF),
            pltpu.VMEM((3, 2, 144, 256), BF),
            pltpu.VMEM((4, 288, HW), BF),
            pltpu.VMEM((2, 256, HW), F32),
            pltpu.VMEM((2, 256, HW), BF),
            pltpu.VMEM((2, 4, 4, 16, HW), BF),
            pltpu.VMEM((2, 4, 16, HW), BF),
            pltpu.VMEM((2, 4, 16, HW), BF),
            pltpu.VMEM((2, 256, HW), BF),
            pltpu.VMEM((2, 2, 16, HW), BF),
            pltpu.VMEM((2, 2, 16, HW), BF),
            pltpu.VMEM((2, 16, HW), BF),
            pltpu.VMEM((2, 16, HW), BF),
            dma((4,)), dma((4,)), dma((4,)), dma((2,)), dma((2,)),
            dma((2, 16)), dma((2, 16)), dma((2, 4)), dma((2, 4)),
            dma((2, 4)), dma((2, 4)), dma((2, 16)), dma((2, 16)),
            dma((4,)), dma((4,)), dma, dma,
        ],
        compiler_params=pltpu.CompilerParams(
            collective_id=0, has_side_effects=True, vmem_limit_bytes=40 * 2**20
        ),
        name="conv_level",
    )(*(pltpu.with_memory_space_constraint(a, pltpu.HBM) for a in (volume, kernel, offset.reshape(1, 16), cotangent)))


def solution(mesh):
    return jax.shard_map(
        per_device,
        mesh=mesh,
        in_specs=(
            P("slab", "chan", None),
            P(None, "chan", None),
            P("chan"),
            P("slab", "chan", None),
        ),
        out_specs=(P("slab", "chan", None), P("slab", "chan", None)),
        check_vma=False,
    )
```

```python
import jax
import jax.numpy as jnp
from jax import lax
from jax.experimental import pallas as pl
from jax.experimental.pallas import tpu as pltpu
from jax.sharding import PartitionSpec as P

H = 16
W = 32
HW = H * W
YN = 4
MESH = pl.DeviceIdType.MESH
BF = jnp.bfloat16
F32 = jnp.float32


def iota(shape, dim):
    return lax.broadcasted_iota(jnp.int32, shape, dim)


def remote(src, dst, ssem, rsem, target):
    return pltpu.make_async_remote_copy(
        src_ref=src, dst_ref=dst, send_sem=ssem, recv_sem=rsem, device_id=target, device_id_type=MESH
    )


def in_grid(dh, dw):
    lane = iota((16, HW), 1)
    h, w = lane // W + dh, lane % W + dw
    return (h >= 0) & (h < H) & (w >= 0) & (w < W)


def moved(x, dh, dw):
    s = dh * W + dw
    if s == 0:
        return x
    return jnp.where(in_grid(dh, dw), pltpu.roll(x, (-s) % HW, 1), 0.0)


def dot(a, b):
    return jnp.dot(a, b, preferred_element_type=F32)


def body(
    vol_hbm, w_hbm, off_hbm, cot_hbm, pooled_ref, grad_ref,
    vbuf, wraw, wturn, off_ref, cot_ref, wsend, wh, cols, acc, part, ysum, zsend, zsum, dp, hsend, hrecv, psend, precv,
    lsem, halo_s, halo_r, sib_s, sib_r, ry_s, ry_r, rz_s, rz_r, az_s, az_r, ay_s, ay_r, bh_s, bh_r, pair_s, pair_r,
):
    slab = lax.axis_index("slab")
    chan = lax.axis_index("chan")
    slabs = lax.axis_size("slab")
    core = chan % 2
    z, y = chan // 2 // YN, chan // 2 % YN
    up = lax.rem(slab + 1, slabs)
    down = lax.rem(slab + slabs - 1, slabs)
    sib = (slab, chan + 1 - 2 * core)

    zs = (z, z + 1 - 2 * lax.rem(z, 2), lax.rem(z + 2, 4), 3 - z)

    first = lax.rem(slab, 4) // 3
    second = 1 - first
    planes = (first, second)

    def yto(dy):
        return (slab, (z * YN + lax.rem(y + dy, YN)) * 2 + core)

    def zto(dz):
        return (slab, (zs[dz] * YN + y) * 2 + core)

    def near(s, b):
        return (s, chan if b == 0 else chan + 1 - 2 * core)

    barrier = pltpu.get_barrier_semaphore()
    pl.semaphore_signal(barrier, inc=1, device_id=sib, device_id_type=MESH)
    has_up = slab < slabs - 1
    has_down = slab > 0
    for s, has in ((up, has_up), (down, has_down)):

        @pl.when(has)
        def _():
            for b in range(2):
                pl.semaphore_signal(barrier, inc=1, device_id=near(s, b), device_id_type=MESH)


    for d in range(1, 4):
        pl.semaphore_signal(barrier, inc=1, device_id=zto(d), device_id_type=MESH)
        pl.semaphore_signal(barrier, inc=1, device_id=yto(d), device_id_type=MESH)

    load_v = pltpu.make_async_copy(vol_hbm, vbuf.at[pl.ds(1, 2), 0], lsem.at[0])
    load_w = pltpu.make_async_copy(w_hbm, wraw, lsem.at[1])
    load_v.start()
    load_w.start()
    load_o = pltpu.make_async_copy(off_hbm, off_ref, lsem.at[2])
    load_c = pltpu.make_async_copy(cot_hbm, cot_ref, lsem.at[3])
    load_o.start()
    load_c.start()
    pl.semaphore_wait(barrier, 7 + 2 * has_up.astype(jnp.int32) + 2 * has_down.astype(jnp.int32))

    def halo(p, b):
        k = 2 * p + b
        slab_to = jnp.where(p == 0, up, down)
        return remote(vol_hbm.at[1 - p], vbuf.at[3 * p, b], halo_s.at[k], halo_r.at[k], near(slab_to, b))

    def sends(p):
        return jnp.where(p == 0, slabs - 1 - slab, slab) > 0

    def receives(p):
        return jnp.where(p == 0, slab, slabs - 1 - slab) > 0

    def both(copy, p, act):
        @pl.when(copy)
        def _():
            for b in range(2):
                act(p, b)

    for p in planes:
        both(sends(p), p, lambda p, b: halo(p, b).start())
    share_v = remote(vol_hbm, vbuf.at[pl.ds(1, 2), 1], sib_s.at[0], sib_r.at[0], sib)
    share_w = remote(wsend, wh.at[:, 1], sib_s.at[1], sib_r.at[1], sib)
    share_v.start()

    load_w.wait()
    wflat = wraw[...].reshape(432, 512)
    o = iota((512, 256), 0)
    r = iota((512, 256), 1)
    zt = 2 * ((z // 2 + r // 128) % 2) + (z % 2 + r // 64) % 2
    place = o - (zt * YN + r // 16 % YN) * 32 - r % 16
    wsend[...] = dot(wflat, (place == 16 * (1 - core)).astype(BF)).astype(BF).reshape(3, 144, 256)
    share_w.start()
    wh[:, 0] = dot(wflat, (place == 16 * core).astype(BF)).astype(BF).reshape(3, 144, 256)
    load_v.wait()

    def columns(plane, b, keep=None):
        x = vbuf[plane, b].astype(F32)
        if keep is not None:
            x = jnp.where(keep, x, 0.0)
        for kh in range(3):
            for kw in range(3):
                row = b * 144 + (kh * 3 + kw) * 16
                cols[plane, row : row + 16] = moved(x, kh - 1, kw - 1).astype(BF)

    columns(1, 0)
    columns(2, 0)
    share_v.wait_recv()
    columns(1, 1)
    columns(2, 1)
    share_w.wait_recv()
    eye = (iota((256, 256), 0) == iota((256, 256), 1)).astype(BF)

    def turned(lo, hi):
        rows = wh[lo:hi].reshape((hi - lo) * 288, 256)
        return lax.dot_general(
            eye, rows, (((1,), (1,)), ((), ())), preferred_element_type=F32
        ).astype(BF)

    inner = cols[1:3].reshape(576, HW)
    acc[0] = dot(turned(1, 3), inner)
    acc[1] = dot(turned(0, 2), inner)
    wturn[0] = turned(0, 1)
    wturn[1] = turned(2, 3)

    def rows(dz, yt):
        return pl.ds(pl.multiple_of(dz * 64 + yt * 16, 16), 16)

    def ry(p, dz, dy):
        k = dz * 4 + dy
        src = part.at[p, rows(dz, lax.rem(y + dy, YN))]
        return remote(src, ysum.at[p, dz, dy], ry_s.at[p, k], ry_r.at[p, k], yto(dy))

    def rz(p, dz):
        return remote(zsend.at[p, dz], zsum.at[p, dz], rz_s.at[p, dz], rz_r.at[p, dz], zto(dz))

    def az(p, dz):
        return remote(dp.at[p, rows(0, y)], dp.at[p, rows(dz, y)], az_s.at[p, dz], az_r.at[p, dz], zto(dz))

    def ay(p, dz, dy):
        k = dz * 4 + dy
        here = dp.at[p, rows(dz, y)]
        return remote(here, here, ay_s.at[p, k], ay_r.at[p, k], yto(dy))

    def ay_arrival(p, dz, dy):
        k = dz * 4 + dy
        here = dp.at[p, rows(dz, lax.rem(y + 4 - dy, YN))]
        return remote(here, here, ay_s.at[p, k], ay_r.at[p, k], yto(dy))

    def ytotal(p, dz):
        t = part[p, rows(dz, y)].astype(F32)
        for dy in (1, 2, 3):
            ry(p, dz, dy).wait_recv()
        for dy in (1, 2, 3):
            t = t + ysum[p, dz, dy].astype(F32)
        return t

    def start_sums(p):
        both(receives(p), p, lambda p, b: halo(p, b).wait_recv())
        for b in range(2):
            columns(3 * p, b, receives(p))
        part[p] = (acc[p] + dot(wturn[p], cols[3 * p])).astype(BF)
        for dz in (3, 2, 1, 0):
            for dy in (2, 1, 3):
                ry(p, dz, dy).start()

    def pass_sums(p):
        for dz in (3, 2, 1):
            zsend[p, dz] = ytotal(p, dz).astype(BF)
            rz(p, dz).start()

    start_sums(first)
    cell = iota((HW, 128), 0)
    coarse = iota((HW, 128), 1)
    pool = (coarse == (cell // (2 * W)) * (W // 2) + (cell % W) // 2).astype(BF)
    cell = iota((128, HW), 1)
    coarse = iota((128, HW), 0)
    unpool = (coarse == (cell // (2 * W)) * (W // 2) + (cell % W) // 2).astype(BF)
    load_o.wait()
    load_c.wait()
    upper = dot(cot_ref[0], unpool) * 0.125
    diag = iota((16, 16), 0) == iota((16, 16), 1)
    offset = jnp.sum(jnp.where(diag, jnp.broadcast_to(off_ref[...], (16, 16)), 0.0), axis=1, keepdims=True)
    def activate(p):
        v = ytotal(p, 0) + offset
        for dz in (1, 2, 3):
            rz(p, dz).wait_recv()
            v = v + zsum[p, dz].astype(F32)
        s = jax.nn.sigmoid(v)
        dp[p, rows(0, y)] = (upper * s * (1.0 + v * (1.0 - s))).astype(BF)
        for dz in (3, 2, 1):
            az(p, dz).start()
        for dy in (2, 1, 3):
            ay(p, 0, dy).start()
        return v * s

    def forward(p, dzs=(1, 2, 3)):
        for dz in dzs:
            az(p, dz).wait_recv()
            for dy in (2, 1, 3):
                ay(p, dz, dy).start()

    start_sums(second)
    pass_sums(first)
    pass_sums(second)
    act = activate(first)
    act = act + activate(second)
    forward(first)
    forward(second)
    act_hi = act.astype(BF)
    act_lo = (act - act_hi.astype(F32)).astype(BF)
    pooled_ref[0] = ((dot(act_hi, pool) + dot(act_lo, pool)) * 0.125).astype(BF)
    share_v.wait_send()
    share_w.wait_send()
    for p in planes:
        both(sends(p), p, lambda p, b: halo(p, b).wait_send())
        for dz in range(4):
            for dy in (1, 2, 3):
                ry(p, dz, dy).wait_send()
        for dz in (1, 2, 3):
            rz(p, dz).wait_send()

    def gathered(prod):
        out = []
        for b in range(2):
            g = jnp.zeros((16, HW), F32)
            for kh in range(3):
                for kw in range(3):
                    row = b * 144 + (kh * 3 + kw) * 16
                    g = g + moved(prod[row : row + 16], 1 - kh, 1 - kw)
            out.append(g)
        return out

    def edge(p, b):
        slab_to = jnp.where(p == 0, down, up)
        return remote(
            hsend.at[p, b], hrecv.at[1 - p, b], bh_s.at[2 * p + b], bh_r.at[2 * (1 - p) + b], near(slab_to, b)
        )

    for p in planes:
        for dz in range(4):
            for dy in (1, 2, 3):
                ay_arrival(p, dz, dy).wait_recv()
        beyond = gathered(dot(wh[2 * p].reshape(288, 256), dp[p]))
        for b in range(2):
            hsend[p, b] = beyond[b].astype(BF)
        both(receives(p), p, lambda p, b: edge(p, b).start())
    for p in planes:
        for dz in range(4):
            for dy in (1, 2, 3):
                ay(p, dz, dy).wait_send()
        for dz in (1, 2, 3):
            az(p, dz).wait_send()
    flat = [wh[k].reshape(288, 256) for k in range(3)]
    dp0, dp1 = dp[0], dp[1]
    g0 = gathered(dot(flat[0], dp1) + dot(flat[1], dp0))
    g1 = gathered(dot(flat[1], dp1) + dot(flat[2], dp0))
    psend[0] = g0[1].astype(BF)
    psend[1] = g1[1].astype(BF)
    pair = remote(psend, precv, pair_s, pair_r, sib)
    pair.start()
    pair.wait_recv()
    g0 = g0[0] + precv[0].astype(F32)
    g1 = g1[0] + precv[1].astype(F32)
    for p in planes:
        both(sends(p), p, lambda p, b: edge(p, b).wait_recv())
    from_down = hrecv[0, 0].astype(F32) + hrecv[0, 1].astype(F32)
    from_up = hrecv[1, 0].astype(F32) + hrecv[1, 1].astype(F32)
    grad_ref[0] = (g0 + jnp.where(slab > 0, from_down, 0.0)).astype(BF)
    grad_ref[1] = (g1 + jnp.where(slab < slabs - 1, from_up, 0.0)).astype(BF)

    pair.wait_send()
    for p in planes:
        both(receives(p), p, lambda p, b: edge(p, b).wait_send())


def per_device(volume, kernel, offset, cotangent):
    vmem = pl.BlockSpec(memory_space=pltpu.VMEM)
    hbm = pl.BlockSpec(memory_space=pl.ANY)
    dma = pltpu.SemaphoreType.DMA
    return pl.pallas_call(
        body,
        out_shape=(
            jax.ShapeDtypeStruct((1, 16, HW // 4), BF),
            jax.ShapeDtypeStruct((2, 16, HW), BF),
        ),
        in_specs=[hbm] * 4,
        out_specs=(vmem, vmem),
        scratch_shapes=[
            pltpu.VMEM((4, 2, 16, HW), BF),
            pltpu.VMEM((27, 16, 512), BF),
            pltpu.VMEM((2, 256, 288), BF),
            pltpu.VMEM((1, 16), F32),
            pltpu.VMEM((1, 16, HW // 4), BF),
            pltpu.VMEM((3, 144, 256), BF),
            pltpu.VMEM((3, 2, 144, 256), BF),
            pltpu.VMEM((4, 288, HW), BF),
            pltpu.VMEM((2, 256, HW), F32),
            pltpu.VMEM((2, 256, HW), BF),
            pltpu.VMEM((2, 4, 4, 16, HW), BF),
            pltpu.VMEM((2, 4, 16, HW), BF),
            pltpu.VMEM((2, 4, 16, HW), BF),
            pltpu.VMEM((2, 256, HW), BF),
            pltpu.VMEM((2, 2, 16, HW), BF),
            pltpu.VMEM((2, 2, 16, HW), BF),
            pltpu.VMEM((2, 16, HW), BF),
            pltpu.VMEM((2, 16, HW), BF),
            dma((4,)), dma((4,)), dma((4,)), dma((2,)), dma((2,)),
            dma((2, 16)), dma((2, 16)), dma((2, 4)), dma((2, 4)),
            dma((2, 4)), dma((2, 4)), dma((2, 16)), dma((2, 16)),
            dma((4,)), dma((4,)), dma, dma,
        ],
        compiler_params=pltpu.CompilerParams(
            collective_id=0, has_side_effects=True, vmem_limit_bytes=40 * 2**20
        ),
        name="conv_level",
    )(*(pltpu.with_memory_space_constraint(a, pltpu.HBM) for a in (volume, kernel, offset.reshape(1, 16), cotangent)))


def solution(mesh):
    return jax.shard_map(
        per_device,
        mesh=mesh,
        in_specs=(
            P("slab", "chan", None),
            P(None, "chan", None),
            P("chan"),
            P("slab", "chan", None),
        ),
        out_specs=(P("slab", "chan", None), P("slab", "chan", None)),
        check_vma=False,
    )
```

```python
import jax
import jax.numpy as jnp
from jax import lax
from jax.experimental import pallas as pl
from jax.experimental.pallas import tpu as pltpu
from jax.sharding import PartitionSpec as P

H = 16
W = 32
HW = H * W
YN = 4
MESH = pl.DeviceIdType.MESH
BF = jnp.bfloat16
F32 = jnp.float32


def iota(shape, dim):
    return lax.broadcasted_iota(jnp.int32, shape, dim)


def remote(src, dst, ssem, rsem, target):
    return pltpu.make_async_remote_copy(
        src_ref=src, dst_ref=dst, send_sem=ssem, recv_sem=rsem, device_id=target, device_id_type=MESH
    )


def in_grid(dh, dw):
    lane = iota((16, HW), 1)
    h, w = lane // W + dh, lane % W + dw
    return (h >= 0) & (h < H) & (w >= 0) & (w < W)


def moved(x, dh, dw):
    s = dh * W + dw
    if s == 0:
        return x
    return jnp.where(in_grid(dh, dw), pltpu.roll(x, (-s) % HW, 1), 0.0)


def dot(a, b):
    return jnp.dot(a, b, preferred_element_type=F32)


def body(
    vol_hbm, w_hbm, off_hbm, cot_hbm, pooled_ref, grad_ref,
    vbuf, wraw, wturn, off_ref, cot_ref, wsend, wh, cols, acc, part, ysum, zsend, zsum, dp, hsend, hrecv, psend, precv,
    lsem, halo_s, halo_r, sib_s, sib_r, ry_s, ry_r, rz_s, rz_r, az_s, az_r, ay_s, ay_r, bh_s, bh_r, pair_s, pair_r,
):
    slab = lax.axis_index("slab")
    chan = lax.axis_index("chan")
    slabs = lax.axis_size("slab")
    core = chan % 2
    z, y = chan // 2 // YN, chan // 2 % YN
    up = lax.rem(slab + 1, slabs)
    down = lax.rem(slab + slabs - 1, slabs)
    sib = (slab, chan + 1 - 2 * core)

    zs = (z, z + 1 - 2 * lax.rem(z, 2), lax.rem(z + 2, 4), 3 - z)

    first = lax.rem(slab, 4) // 2
    second = 1 - first
    planes = (first, second)

    def yto(dy):
        return (slab, (z * YN + lax.rem(y + dy, YN)) * 2 + core)

    def zto(dz):
        return (slab, (zs[dz] * YN + y) * 2 + core)

    def near(s, b):
        return (s, chan if b == 0 else chan + 1 - 2 * core)

    load_v = pltpu.make_async_copy(vol_hbm, vbuf.at[pl.ds(1, 2), 0], lsem.at[0])
    load_v.start()
    barrier = pltpu.get_barrier_semaphore()
    pl.semaphore_signal(barrier, inc=1, device_id=sib, device_id_type=MESH)
    has_up = slab < slabs - 1
    has_down = slab > 0
    for s, has in ((up, has_up), (down, has_down)):

        @pl.when(has)
        def _():
            for b in range(2):
                pl.semaphore_signal(barrier, inc=1, device_id=near(s, b), device_id_type=MESH)


    for d in range(1, 4):
        pl.semaphore_signal(barrier, inc=1, device_id=zto(d), device_id_type=MESH)
        pl.semaphore_signal(barrier, inc=1, device_id=yto(d), device_id_type=MESH)

    load_w = pltpu.make_async_copy(w_hbm, wraw, lsem.at[1])
    load_w.start()
    load_o = pltpu.make_async_copy(off_hbm, off_ref, lsem.at[2])
    load_c = pltpu.make_async_copy(cot_hbm, cot_ref, lsem.at[3])
    load_o.start()
    load_c.start()
    pl.semaphore_wait(barrier, 7 + 2 * has_up.astype(jnp.int32) + 2 * has_down.astype(jnp.int32))

    load_v.wait()

    def halo(p, b):
        k = 2 * p + b
        slab_to = jnp.where(p == 0, up, down)
        return remote(vbuf.at[2 - p, 0], vbuf.at[3 * p, b], halo_s.at[k], halo_r.at[k], near(slab_to, b))

    def sends(p):
        return jnp.where(p == 0, slabs - 1 - slab, slab) > 0

    def receives(p):
        return jnp.where(p == 0, slab, slabs - 1 - slab) > 0

    def both(copy, p, act):
        @pl.when(copy)
        def _():
            for b in range(2):
                act(p, b)

    for p in planes:
        both(sends(p), p, lambda p, b: halo(p, b).start())
    share_v = remote(vol_hbm, vbuf.at[pl.ds(1, 2), 1], sib_s.at[0], sib_r.at[0], sib)
    share_w = remote(wsend, wh.at[:, 1], sib_s.at[1], sib_r.at[1], sib)
    share_v.start()

    load_w.wait()
    wflat = wraw[...].reshape(432, 512)
    o = iota((512, 256), 0)
    r = iota((512, 256), 1)
    zt = 2 * ((z // 2 + r // 128) % 2) + (z % 2 + r // 64) % 2
    place = o - (zt * YN + r // 16 % YN) * 32 - r % 16
    wsend[...] = dot(wflat, (place == 16 * (1 - core)).astype(BF)).astype(BF).reshape(3, 144, 256)
    share_w.start()
    wh[:, 0] = dot(wflat, (place == 16 * core).astype(BF)).astype(BF).reshape(3, 144, 256)
    def columns(plane, b, keep=None):
        x = vbuf[plane, b].astype(F32)
        if keep is not None:
            x = jnp.where(keep, x, 0.0)
        for kh in range(3):
            for kw in range(3):
                row = b * 144 + (kh * 3 + kw) * 16
                cols[plane, row : row + 16] = moved(x, kh - 1, kw - 1).astype(BF)

    columns(1, 0)
    columns(2, 0)
    share_v.wait_recv()
    columns(1, 1)
    columns(2, 1)
    share_w.wait_recv()
    eye = (iota((256, 256), 0) == iota((256, 256), 1)).astype(BF)

    def turned(lo, hi):
        rows = wh[lo:hi].reshape((hi - lo) * 288, 256)
        return lax.dot_general(
            eye, rows, (((1,), (1,)), ((), ())), preferred_element_type=F32
        ).astype(BF)

    inner = cols[1:3].reshape(576, HW)
    acc[0] = dot(turned(1, 3), inner)
    acc[1] = dot(turned(0, 2), inner)
    wturn[0] = turned(0, 1)
    wturn[1] = turned(2, 3)

    def rows(dz, yt):
        return pl.ds(pl.multiple_of(dz * 64 + yt * 16, 16), 16)

    def ry(p, dz, dy):
        k = dz * 4 + dy
        src = part.at[p, rows(dz, lax.rem(y + dy, YN))]
        return remote(src, ysum.at[p, dz, dy], ry_s.at[p, k], ry_r.at[p, k], yto(dy))

    def rz(p, dz):
        return remote(zsend.at[p, dz], zsum.at[p, dz], rz_s.at[p, dz], rz_r.at[p, dz], zto(dz))

    def az(p, dz):
        return remote(dp.at[p, rows(0, y)], dp.at[p, rows(dz, y)], az_s.at[p, dz], az_r.at[p, dz], zto(dz))

    def ay(p, dz, dy):
        k = dz * 4 + dy
        here = dp.at[p, rows(dz, y)]
        return remote(here, here, ay_s.at[p, k], ay_r.at[p, k], yto(dy))

    def ay_arrival(p, dz, dy):
        k = dz * 4 + dy
        here = dp.at[p, rows(dz, lax.rem(y + 4 - dy, YN))]
        return remote(here, here, ay_s.at[p, k], ay_r.at[p, k], yto(dy))

    def ytotal(p, dz):
        t = part[p, rows(dz, y)].astype(F32)
        for dy in (1, 2, 3):
            ry(p, dz, dy).wait_recv()
        for dy in (1, 2, 3):
            t = t + ysum[p, dz, dy].astype(F32)
        return t

    def start_sums(p):
        both(receives(p), p, lambda p, b: halo(p, b).wait_recv())
        for b in range(2):
            columns(3 * p, b, receives(p))
        part[p] = (acc[p] + dot(wturn[p], cols[3 * p])).astype(BF)
        for dz in (3, 2, 1, 0):
            for dy in (2, 1, 3):
                ry(p, dz, dy).start()

    def pass_sums(p):
        for dz in (3, 2, 1):
            zsend[p, dz] = ytotal(p, dz).astype(BF)
            rz(p, dz).start()

    start_sums(first)
    cell = iota((HW, 128), 0)
    coarse = iota((HW, 128), 1)
    pool = (coarse == (cell // (2 * W)) * (W // 2) + (cell % W) // 2).astype(BF)
    cell = iota((128, HW), 1)
    coarse = iota((128, HW), 0)
    unpool = (coarse == (cell // (2 * W)) * (W // 2) + (cell % W) // 2).astype(BF)
    load_o.wait()
    load_c.wait()
    upper = dot(cot_ref[0], unpool) * 0.125
    diag = iota((16, 16), 0) == iota((16, 16), 1)
    offset = jnp.sum(jnp.where(diag, jnp.broadcast_to(off_ref[...], (16, 16)), 0.0), axis=1, keepdims=True)
    def activate(p):
        v = ytotal(p, 0) + offset
        for dz in (1, 2, 3):
            rz(p, dz).wait_recv()
            v = v + zsum[p, dz].astype(F32)
        s = jax.nn.sigmoid(v)
        dp[p, rows(0, y)] = (upper * s * (1.0 + v * (1.0 - s))).astype(BF)
        for dz in (3, 2, 1):
            az(p, dz).start()
        for dy in (2, 1, 3):
            ay(p, 0, dy).start()
        return v * s

    def forward(p, dzs=(1, 2, 3)):
        for dz in dzs:
            az(p, dz).wait_recv()
            for dy in (2, 1, 3):
                ay(p, dz, dy).start()

    start_sums(second)
    pass_sums(first)
    pass_sums(second)
    act = activate(first)
    act = act + activate(second)
    forward(first)
    forward(second)
    act_hi = act.astype(BF)
    act_lo = (act - act_hi.astype(F32)).astype(BF)
    pooled_ref[0] = ((dot(act_hi, pool) + dot(act_lo, pool)) * 0.125).astype(BF)
    share_v.wait_send()
    share_w.wait_send()
    for p in planes:
        both(sends(p), p, lambda p, b: halo(p, b).wait_send())
        for dz in range(4):
            for dy in (1, 2, 3):
                ry(p, dz, dy).wait_send()
        for dz in (1, 2, 3):
            rz(p, dz).wait_send()

    def gathered(prod):
        out = []
        for b in range(2):
            g = jnp.zeros((16, HW), F32)
            for kh in range(3):
                for kw in range(3):
                    row = b * 144 + (kh * 3 + kw) * 16
                    g = g + moved(prod[row : row + 16], 1 - kh, 1 - kw)
            out.append(g)
        return out

    def edge(p, b):
        slab_to = jnp.where(p == 0, down, up)
        return remote(
            hsend.at[p, b], hrecv.at[1 - p, b], bh_s.at[2 * p + b], bh_r.at[2 * (1 - p) + b], near(slab_to, b)
        )

    for p in planes:
        for dz in range(4):
            for dy in (1, 2, 3):
                ay_arrival(p, dz, dy).wait_recv()
        beyond = gathered(dot(wh[2 * p].reshape(288, 256), dp[p]))
        for b in range(2):
            hsend[p, b] = beyond[b].astype(BF)
        both(receives(p), p, lambda p, b: edge(p, b).start())
    for p in planes:
        for dz in range(4):
            for dy in (1, 2, 3):
                ay(p, dz, dy).wait_send()
        for dz in (1, 2, 3):
            az(p, dz).wait_send()
    flat = [wh[k].reshape(288, 256) for k in range(3)]
    dp0, dp1 = dp[0], dp[1]
    g0 = gathered(dot(flat[0], dp1) + dot(flat[1], dp0))
    g1 = gathered(dot(flat[1], dp1) + dot(flat[2], dp0))
    psend[0] = g0[1].astype(BF)
    psend[1] = g1[1].astype(BF)
    pair = remote(psend, precv, pair_s, pair_r, sib)
    pair.start()
    pair.wait_recv()
    g0 = g0[0] + precv[0].astype(F32)
    g1 = g1[0] + precv[1].astype(F32)
    for p in planes:
        both(sends(p), p, lambda p, b: edge(p, b).wait_recv())
    from_down = hrecv[0, 0].astype(F32) + hrecv[0, 1].astype(F32)
    from_up = hrecv[1, 0].astype(F32) + hrecv[1, 1].astype(F32)
    grad_ref[0] = (g0 + jnp.where(slab > 0, from_down, 0.0)).astype(BF)
    grad_ref[1] = (g1 + jnp.where(slab < slabs - 1, from_up, 0.0)).astype(BF)

    pair.wait_send()
    for p in planes:
        both(receives(p), p, lambda p, b: edge(p, b).wait_send())


def per_device(volume, kernel, offset, cotangent):
    vmem = pl.BlockSpec(memory_space=pltpu.VMEM)
    hbm = pl.BlockSpec(memory_space=pl.ANY)
    dma = pltpu.SemaphoreType.DMA
    return pl.pallas_call(
        body,
        out_shape=(
            jax.ShapeDtypeStruct((1, 16, HW // 4), BF),
            jax.ShapeDtypeStruct((2, 16, HW), BF),
        ),
        in_specs=[hbm] * 4,
        out_specs=(vmem, vmem),
        scratch_shapes=[
            pltpu.VMEM((4, 2, 16, HW), BF),
            pltpu.VMEM((27, 16, 512), BF),
            pltpu.VMEM((2, 256, 288), BF),
            pltpu.VMEM((1, 16), F32),
            pltpu.VMEM((1, 16, HW // 4), BF),
            pltpu.VMEM((3, 144, 256), BF),
            pltpu.VMEM((3, 2, 144, 256), BF),
            pltpu.VMEM((4, 288, HW), BF),
            pltpu.VMEM((2, 256, HW), F32),
            pltpu.VMEM((2, 256, HW), BF),
            pltpu.VMEM((2, 4, 4, 16, HW), BF),
            pltpu.VMEM((2, 4, 16, HW), BF),
            pltpu.VMEM((2, 4, 16, HW), BF),
            pltpu.VMEM((2, 256, HW), BF),
            pltpu.VMEM((2, 2, 16, HW), BF),
            pltpu.VMEM((2, 2, 16, HW), BF),
            pltpu.VMEM((2, 16, HW), BF),
            pltpu.VMEM((2, 16, HW), BF),
            dma((4,)), dma((4,)), dma((4,)), dma((2,)), dma((2,)),
            dma((2, 16)), dma((2, 16)), dma((2, 4)), dma((2, 4)),
            dma((2, 4)), dma((2, 4)), dma((2, 16)), dma((2, 16)),
            dma((4,)), dma((4,)), dma, dma,
        ],
        compiler_params=pltpu.CompilerParams(
            collective_id=0, has_side_effects=True, vmem_limit_bytes=40 * 2**20
        ),
        name="conv_level",
    )(*(pltpu.with_memory_space_constraint(a, pltpu.HBM) for a in (volume, kernel, offset.reshape(1, 16), cotangent)))


def solution(mesh):
    return jax.shard_map(
        per_device,
        mesh=mesh,
        in_specs=(
            P("slab", "chan", None),
            P(None, "chan", None),
            P("chan"),
            P("slab", "chan", None),
        ),
        out_specs=(P("slab", "chan", None), P("slab", "chan", None)),
        check_vma=False,
    )
```

```python
import jax
import jax.numpy as jnp
from jax import lax
from jax.experimental import pallas as pl
from jax.experimental.pallas import tpu as pltpu
from jax.sharding import PartitionSpec as P

H = 16
W = 32
HW = H * W
YN = 4
MESH = pl.DeviceIdType.MESH
BF = jnp.bfloat16
F32 = jnp.float32


def iota(shape, dim):
    return lax.broadcasted_iota(jnp.int32, shape, dim)


def remote(src, dst, ssem, rsem, target):
    return pltpu.make_async_remote_copy(
        src_ref=src, dst_ref=dst, send_sem=ssem, recv_sem=rsem, device_id=target, device_id_type=MESH
    )


def in_grid(dh, dw):
    lane = iota((16, HW), 1)
    h, w = lane // W + dh, lane % W + dw
    return (h >= 0) & (h < H) & (w >= 0) & (w < W)


def moved(x, dh, dw):
    s = dh * W + dw
    if s == 0:
        return x
    return jnp.where(in_grid(dh, dw), pltpu.roll(x, (-s) % HW, 1), 0.0)


def dot(a, b):
    return jnp.dot(a, b, preferred_element_type=F32)


def body(
    vol_hbm, w_hbm, off_hbm, cot_hbm, pooled_ref, grad_ref,
    vbuf, wraw, wturn, off_ref, cot_ref, wsend, wh, cols, acc, part, ysum, zsend, zsum, dp, hsend, hrecv, psend, precv,
    lsem, halo_s, halo_r, sib_s, sib_r, ry_s, ry_r, rz_s, rz_r, az_s, az_r, ay_s, ay_r, bh_s, bh_r, pair_s, pair_r,
):
    slab = lax.axis_index("slab")
    chan = lax.axis_index("chan")
    slabs = lax.axis_size("slab")
    core = chan % 2
    z, y = chan // 2 // YN, chan // 2 % YN
    up = lax.rem(slab + 1, slabs)
    down = lax.rem(slab + slabs - 1, slabs)
    sib = (slab, chan + 1 - 2 * core)

    zs = (z, z + 1 - 2 * lax.rem(z, 2), lax.rem(z + 2, 4), 3 - z)

    first = lax.rem(slab, 4) // 2
    second = 1 - first
    planes = (first, second)

    def yto(dy):
        return (slab, (z * YN + lax.rem(y + dy, YN)) * 2 + core)

    def zto(dz):
        return (slab, (zs[dz] * YN + y) * 2 + core)

    def near(s, b):
        return (s, chan if b == 0 else chan + 1 - 2 * core)

    load_v = pltpu.make_async_copy(vol_hbm, vbuf.at[pl.ds(1, 2), 0], lsem.at[0])
    load_v.start()
    barrier = pltpu.get_barrier_semaphore()
    pl.semaphore_signal(barrier, inc=1, device_id=sib, device_id_type=MESH)
    has_up = slab < slabs - 1
    has_down = slab > 0
    for s, has in ((up, has_up), (down, has_down)):

        @pl.when(has)
        def _():
            for b in range(2):
                pl.semaphore_signal(barrier, inc=1, device_id=near(s, b), device_id_type=MESH)


    for d in range(1, 4):
        pl.semaphore_signal(barrier, inc=1, device_id=zto(d), device_id_type=MESH)
        pl.semaphore_signal(barrier, inc=1, device_id=yto(d), device_id_type=MESH)

    load_w = pltpu.make_async_copy(w_hbm, wraw, lsem.at[1])
    load_w.start()
    load_o = pltpu.make_async_copy(off_hbm, off_ref, lsem.at[2])
    load_c = pltpu.make_async_copy(cot_hbm, cot_ref, lsem.at[3])
    load_o.start()
    load_c.start()
    pl.semaphore_wait(barrier, 7 + 2 * has_up.astype(jnp.int32) + 2 * has_down.astype(jnp.int32))

    load_v.wait()

    def halo(p, b):
        k = 2 * p + b
        slab_to = jnp.where(p == 0, up, down)
        return remote(vbuf.at[2 - p, 0], vbuf.at[3 * p, b], halo_s.at[k], halo_r.at[k], near(slab_to, b))

    def sends(p):
        return jnp.where(p == 0, slabs - 1 - slab, slab) > 0

    def receives(p):
        return jnp.where(p == 0, slab, slabs - 1 - slab) > 0

    def both(copy, p, act):
        @pl.when(copy)
        def _():
            for b in range(2):
                act(p, b)

    for p in planes:
        both(sends(p), p, lambda p, b: halo(p, b).start())
    share_v = remote(vol_hbm, vbuf.at[pl.ds(1, 2), 1], sib_s.at[0], sib_r.at[0], sib)
    share_w = remote(wsend, wh.at[:, 1], sib_s.at[1], sib_r.at[1], sib)
    share_v.start()

    load_w.wait()
    wflat = wraw[...].reshape(432, 512)
    o = iota((512, 256), 0)
    r = iota((512, 256), 1)
    zt = 2 * ((z // 2 + r // 128) % 2) + (z % 2 + r // 64) % 2
    place = o - (zt * YN + r // 16 % YN) * 32 - r % 16
    wsend[...] = dot(wflat, (place == 16 * (1 - core)).astype(BF)).astype(BF).reshape(3, 144, 256)
    share_w.start()
    wh[:, 0] = dot(wflat, (place == 16 * core).astype(BF)).astype(BF).reshape(3, 144, 256)
    def columns(plane, b, keep=None):
        x = vbuf[plane, b].astype(F32)
        if keep is not None:
            x = jnp.where(keep, x, 0.0)
        for kh in range(3):
            for kw in range(3):
                row = b * 144 + (kh * 3 + kw) * 16
                cols[plane, row : row + 16] = moved(x, kh - 1, kw - 1).astype(BF)

    columns(1, 0)
    columns(2, 0)
    share_v.wait_recv()
    columns(1, 1)
    columns(2, 1)
    share_w.wait_recv()
    eye = (iota((256, 256), 0) == iota((256, 256), 1)).astype(BF)

    def turned(lo, hi):
        rows = wh[lo:hi].reshape((hi - lo) * 288, 256)
        return lax.dot_general(
            eye, rows, (((1,), (1,)), ((), ())), preferred_element_type=F32
        ).astype(BF)

    inner = cols[1:3].reshape(576, HW)
    acc[0] = dot(turned(1, 3), inner)
    acc[1] = dot(turned(0, 2), inner)
    wturn[0] = turned(0, 1)
    wturn[1] = turned(2, 3)

    def rows(dz, yt):
        return pl.ds(pl.multiple_of(dz * 64 + yt * 16, 16), 16)

    def ry(p, dz, dy):
        k = dz * 4 + dy
        src = part.at[p, rows(dz, lax.rem(y + dy, YN))]
        return remote(src, ysum.at[p, dz, dy], ry_s.at[p, k], ry_r.at[p, k], yto(dy))

    def rz(p, dz):
        return remote(zsend.at[p, dz], zsum.at[p, dz], rz_s.at[p, dz], rz_r.at[p, dz], zto(dz))

    def az(p, dz):
        return remote(dp.at[p, rows(0, y)], dp.at[p, rows(dz, y)], az_s.at[p, dz], az_r.at[p, dz], zto(dz))

    def ay(p, dz, dy):
        k = dz * 4 + dy
        here = dp.at[p, rows(dz, y)]
        return remote(here, here, ay_s.at[p, k], ay_r.at[p, k], yto(dy))

    def ay_arrival(p, dz, dy):
        k = dz * 4 + dy
        here = dp.at[p, rows(dz, lax.rem(y + 4 - dy, YN))]
        return remote(here, here, ay_s.at[p, k], ay_r.at[p, k], yto(dy))

    def ytotal(p, dz):
        t = part[p, rows(dz, y)].astype(F32)
        for dy in (1, 2, 3):
            ry(p, dz, dy).wait_recv()
        for dy in (1, 2, 3):
            t = t + ysum[p, dz, dy].astype(F32)
        return t

    def start_sums(p):
        for b in range(2):

            @pl.when(receives(p))
            def _():
                halo(p, b).wait_recv()

            columns(3 * p, b, receives(p))
        part[p] = (acc[p] + dot(wturn[p], cols[3 * p])).astype(BF)
        for dz in (3, 2, 1, 0):
            for dy in (2, 1, 3):
                ry(p, dz, dy).start()

    def pass_sums(p):
        for dz in (3, 2, 1):
            zsend[p, dz] = ytotal(p, dz).astype(BF)
            rz(p, dz).start()

    start_sums(first)
    cell = iota((HW, 128), 0)
    coarse = iota((HW, 128), 1)
    pool = (coarse == (cell // (2 * W)) * (W // 2) + (cell % W) // 2).astype(BF)
    cell = iota((128, HW), 1)
    coarse = iota((128, HW), 0)
    unpool = (coarse == (cell // (2 * W)) * (W // 2) + (cell % W) // 2).astype(BF)
    load_o.wait()
    load_c.wait()
    upper = dot(cot_ref[0], unpool) * 0.125
    diag = iota((16, 16), 0) == iota((16, 16), 1)
    offset = jnp.sum(jnp.where(diag, jnp.broadcast_to(off_ref[...], (16, 16)), 0.0), axis=1, keepdims=True)
    def activate(p):
        v = ytotal(p, 0) + offset
        for dz in (1, 2, 3):
            rz(p, dz).wait_recv()
            v = v + zsum[p, dz].astype(F32)
        s = jax.nn.sigmoid(v)
        dp[p, rows(0, y)] = (upper * s * (1.0 + v * (1.0 - s))).astype(BF)
        for dz in (3, 2, 1):
            az(p, dz).start()
        for dy in (2, 1, 3):
            ay(p, 0, dy).start()
        return v * s

    def forward(p, dzs=(1, 2, 3)):
        for dz in dzs:
            az(p, dz).wait_recv()
            for dy in (2, 1, 3):
                ay(p, dz, dy).start()

    start_sums(second)
    pass_sums(first)
    pass_sums(second)
    act = activate(first)
    act = act + activate(second)
    forward(first)
    forward(second)
    act_hi = act.astype(BF)
    act_lo = (act - act_hi.astype(F32)).astype(BF)
    pooled_ref[0] = ((dot(act_hi, pool) + dot(act_lo, pool)) * 0.125).astype(BF)
    share_v.wait_send()
    share_w.wait_send()
    for p in planes:
        both(sends(p), p, lambda p, b: halo(p, b).wait_send())
        for dz in range(4):
            for dy in (1, 2, 3):
                ry(p, dz, dy).wait_send()
        for dz in (1, 2, 3):
            rz(p, dz).wait_send()

    def gathered(prod):
        out = []
        for b in range(2):
            g = jnp.zeros((16, HW), F32)
            for kh in range(3):
                for kw in range(3):
                    row = b * 144 + (kh * 3 + kw) * 16
                    g = g + moved(prod[row : row + 16], 1 - kh, 1 - kw)
            out.append(g)
        return out

    def edge(p, b):
        slab_to = jnp.where(p == 0, down, up)
        return remote(
            hsend.at[p, b], hrecv.at[1 - p, b], bh_s.at[2 * p + b], bh_r.at[2 * (1 - p) + b], near(slab_to, b)
        )

    for p in planes:
        for dz in range(4):
            for dy in (1, 2, 3):
                ay_arrival(p, dz, dy).wait_recv()
        beyond = gathered(dot(wh[2 * p].reshape(288, 256), dp[p]))
        for b in range(2):
            hsend[p, b] = beyond[b].astype(BF)
        both(receives(p), p, lambda p, b: edge(p, b).start())
    for p in planes:
        for dz in range(4):
            for dy in (1, 2, 3):
                ay(p, dz, dy).wait_send()
        for dz in (1, 2, 3):
            az(p, dz).wait_send()
    flat = [wh[k].reshape(288, 256) for k in range(3)]
    dp0, dp1 = dp[0], dp[1]
    g0 = gathered(dot(flat[0], dp1) + dot(flat[1], dp0))
    g1 = gathered(dot(flat[1], dp1) + dot(flat[2], dp0))
    psend[0] = g0[1].astype(BF)
    psend[1] = g1[1].astype(BF)
    pair = remote(psend, precv, pair_s, pair_r, sib)
    pair.start()
    pair.wait_recv()
    g0 = g0[0] + precv[0].astype(F32)
    g1 = g1[0] + precv[1].astype(F32)
    for p in planes:
        both(sends(p), p, lambda p, b: edge(p, b).wait_recv())
    from_down = hrecv[0, 0].astype(F32) + hrecv[0, 1].astype(F32)
    from_up = hrecv[1, 0].astype(F32) + hrecv[1, 1].astype(F32)
    grad_ref[0] = (g0 + jnp.where(slab > 0, from_down, 0.0)).astype(BF)
    grad_ref[1] = (g1 + jnp.where(slab < slabs - 1, from_up, 0.0)).astype(BF)

    pair.wait_send()
    for p in planes:
        both(receives(p), p, lambda p, b: edge(p, b).wait_send())


def per_device(volume, kernel, offset, cotangent):
    vmem = pl.BlockSpec(memory_space=pltpu.VMEM)
    hbm = pl.BlockSpec(memory_space=pl.ANY)
    dma = pltpu.SemaphoreType.DMA
    return pl.pallas_call(
        body,
        out_shape=(
            jax.ShapeDtypeStruct((1, 16, HW // 4), BF),
            jax.ShapeDtypeStruct((2, 16, HW), BF),
        ),
        in_specs=[hbm] * 4,
        out_specs=(vmem, vmem),
        scratch_shapes=[
            pltpu.VMEM((4, 2, 16, HW), BF),
            pltpu.VMEM((27, 16, 512), BF),
            pltpu.VMEM((2, 256, 288), BF),
            pltpu.VMEM((1, 16), F32),
            pltpu.VMEM((1, 16, HW // 4), BF),
            pltpu.VMEM((3, 144, 256), BF),
            pltpu.VMEM((3, 2, 144, 256), BF),
            pltpu.VMEM((4, 288, HW), BF),
            pltpu.VMEM((2, 256, HW), F32),
            pltpu.VMEM((2, 256, HW), BF),
            pltpu.VMEM((2, 4, 4, 16, HW), BF),
            pltpu.VMEM((2, 4, 16, HW), BF),
            pltpu.VMEM((2, 4, 16, HW), BF),
            pltpu.VMEM((2, 256, HW), BF),
            pltpu.VMEM((2, 2, 16, HW), BF),
            pltpu.VMEM((2, 2, 16, HW), BF),
            pltpu.VMEM((2, 16, HW), BF),
            pltpu.VMEM((2, 16, HW), BF),
            dma((4,)), dma((4,)), dma((4,)), dma((2,)), dma((2,)),
            dma((2, 16)), dma((2, 16)), dma((2, 4)), dma((2, 4)),
            dma((2, 4)), dma((2, 4)), dma((2, 16)), dma((2, 16)),
            dma((4,)), dma((4,)), dma, dma,
        ],
        compiler_params=pltpu.CompilerParams(
            collective_id=0, has_side_effects=True, vmem_limit_bytes=40 * 2**20
        ),
        name="conv_level",
    )(*(pltpu.with_memory_space_constraint(a, pltpu.HBM) for a in (volume, kernel, offset.reshape(1, 16), cotangent)))


def solution(mesh):
    return jax.shard_map(
        per_device,
        mesh=mesh,
        in_specs=(
            P("slab", "chan", None),
            P(None, "chan", None),
            P("chan"),
            P("slab", "chan", None),
        ),
        out_specs=(P("slab", "chan", None), P("slab", "chan", None)),
        check_vma=False,
    )
```
